32 devices in a mesh: row: 8 (over z, core), col: 4 (over y, x).
Axes of the slice: x: 2, y: 2, z: 4, core: 2. Of those that a mesh axis runs over, the one named last changes fastest.
Arguments:
- queries: bfloat16 [4096, 2048], P(('row', 'col')), may hold values from -6 to 6
- keys: bfloat16 [4096, 256], P(('row', 'col')), may hold values from -30 to 30
- values: bfloat16 [4096, 256], P(('row', 'col')), may hold values from -6 to 6
Outputs:
- attended: bfloat16 [4096, 2048], P(('row', 'col'))
The draws below stay inside these ranges and needn't reach their ends.
All inputs are finite; a program needn't handle non-finite values.
Results may differ from the reference program's by a relative error of at most 0.0057.
Values sent between devices are 32-bit elements; how exact they have to be, the bound alone decides.
A program may use at most 128 MiB of HBM per device.

```python
import math
import jax
import jax.numpy as jnp
import numpy as np
from jax import lax

HD = 64
KV = 4
QH = 32
TOK_DEV = 128
F = 2080
TOKENS = 4096


def draw_keys(key, part):
    noise_key, row_key, region_key = jax.random.split(key, 3)
    base = jax.random.truncated_normal(noise_key, -4.0, 4.0, (TOKENS, KV * HD), jnp.float32)
    row_scale = jnp.exp(jax.random.uniform(row_key, (TOKENS, 1), jnp.float32, 0.0, math.log(3.0)))
    regions = TOKENS // (4 * TOK_DEV)
    region_scale = jnp.exp(jax.random.uniform(region_key, (regions, 1), jnp.float32, math.log(0.5), math.log(2.0)))
    region_scale = jnp.repeat(region_scale, 4 * TOK_DEV, axis=0, total_repeat_length=TOKENS)
    return (base * row_scale * region_scale).astype(jnp.bfloat16)


def levels(rng, shape, shards, smallest, largest):
    level, own = 1.0, jax.random.fold_in(rng, 6)
    for dim, parts in shards:
        steps = jnp.exp(jax.random.uniform(jax.random.fold_in(own, dim), (parts,), jnp.float32, smallest / len(shards), largest / len(shards)))
        level = level * jnp.repeat(steps, shape[dim] // parts).reshape([-1 if axis == dim else 1 for axis in range(len(shape))])
    return level


def scatter_about(rng, extent, scale, reach, cuts=(), held_as=jnp.bfloat16):
    result = jax.random.normal(rng, extent, jnp.float32) * scale
    if len(cuts) > 0:
        result = levels(rng, extent, cuts, -0.22, 0.18) * result
    return jnp.clip(result, min=-reach, max=reach).astype(held_as)


def setup_inputs(seed: int = 0) -> dict:
    streams_of = jax.random.split(jax.random.key(seed), 4)
    return {
        "queries": scatter_about(streams_of[0], (TOKENS, QH * HD), 1.0, 6.0, ((0, 32),)),
        "keys": draw_keys(jax.random.fold_in(streams_of[3], 71), 0),
        "values": scatter_about(streams_of[2], (TOKENS, KV * HD), 1.0, 6.0, ((0, 32),)),
    }


def expand(field):
    width = field.shape[1]
    pieces = []
    for leading in range(width):
        factor = np.full((width - leading,), math.sqrt(2.0), np.float32)
        factor[0] = 1.0
        piece = field[:, leading:leading + 1, :] * field[:, leading:, :]
        pieces.append(piece * jnp.asarray(factor, jnp.float32)[None, :, None])
    return jnp.concatenate(pieces, axis=1)

def rounded(field):
    return lax.optimization_barrier(field.astype(jnp.bfloat16)).astype(jnp.float32)

def summarize(block_keys, block_values):
    rows_here = block_keys.shape[0]
    keys_split = block_keys.reshape(rows_here, KV, HD).astype(jnp.float32)
    values_split = block_values.reshape(rows_here, KV, HD).astype(jnp.float32)
    key_feats = rounded(expand(jnp.transpose(keys_split, (1, 2, 0))))
    state = jnp.einsum('kft,tkv->fkv', key_feats, values_split).reshape(F, KV * HD)
    count = jnp.einsum('kft->fk', key_feats)
    return (state, count)

def attend_block(block_queries, block_keys, block_values, carried_state, carried_count):
    rows_here = block_queries.shape[0]
    per_group = QH // KV
    score_scale = 1.0 / math.sqrt(HD)
    query_split = block_queries.reshape(rows_here, KV, per_group, HD)
    keys_split = block_keys.reshape(rows_here, KV, HD)
    values_split = block_values.reshape(rows_here, KV, HD)
    causal = lax.broadcasted_iota(jnp.int32, (rows_here, rows_here), 0) >= lax.broadcasted_iota(jnp.int32, (rows_here, rows_here), 1)

    def one_head(head_index):
        query_group = lax.dynamic_index_in_dim(query_split, head_index, 1, keepdims=False).astype(jnp.float32)
        key_head = lax.dynamic_index_in_dim(keys_split, head_index, 1, keepdims=False).astype(jnp.float32)
        value_head = lax.dynamic_index_in_dim(values_split, head_index, 1, keepdims=False).astype(jnp.float32)
        state_head = lax.dynamic_slice_in_dim(carried_state, (head_index * HD).astype(jnp.int32), HD, 1).astype(jnp.float32)
        count_head = lax.dynamic_index_in_dim(carried_count, head_index, 1, keepdims=False).astype(jnp.float32)
        query_feats = rounded(expand(jnp.transpose(query_group * score_scale, (1, 2, 0))))
        far_num = jnp.einsum('gft,fv->gtv', query_feats, state_head)
        far_den = jnp.einsum('gft,f->gt', query_feats, count_head)
        scores = jnp.einsum('tgd,ud->gtu', query_group, key_head) * score_scale
        weights = jnp.where(causal[None], scores * scores, 0.0)
        near_den = lax.optimization_barrier(jnp.sum(weights, axis=-1))
        near_num = jnp.einsum('gtu,ud->gtd', rounded(weights), value_head)
        ratio = (far_num + near_num) / jnp.maximum(far_den + near_den, 1.0)[..., None]
        return jnp.transpose(ratio, (1, 0, 2)).reshape(rows_here, per_group * HD)
    heads = lax.map(one_head, jnp.arange(KV, dtype=jnp.int32))
    return jnp.transpose(heads, (1, 0, 2)).reshape(rows_here, QH * HD).astype(jnp.bfloat16)

def block_step(carry, inputs):
    total_state, total_count = carry
    block_queries, block_keys, block_values = inputs
    outputs = attend_block(block_queries, block_keys, block_values, total_state.astype(jnp.bfloat16), total_count.astype(jnp.bfloat16))
    state, count = summarize(block_keys, block_values)
    return ((total_state + state, total_count + count), outputs)

def reference(queries, keys, values):
    blocks = TOKENS // TOK_DEV
    start = (jnp.zeros((F, KV * HD), jnp.float32), jnp.zeros((F, KV), jnp.float32))
    inputs = (queries.reshape(blocks, TOK_DEV, QH * HD), keys.reshape(blocks, TOK_DEV, KV * HD), values.reshape(blocks, TOK_DEV, KV * HD))
    final, outputs = lax.scan(block_step, start, inputs)
    return outputs.reshape(TOKENS, QH * HD)
```

```python
import jax
import jax.numpy as jnp
from jax import lax
from jax.experimental import pallas as pl
from jax.experimental.pallas import tpu as pltpu
from jax.sharding import PartitionSpec as P

HD = 64
KV = 4
QH = 32
PAIRS = QH // KV // 2
LANES = 2 * HD


def paired(tile, odd):
    low = lax.broadcasted_iota(jnp.int32, tile.shape, 1) < HD
    other = pltpu.roll(tile, HD, 1)
    zero = jnp.zeros_like(tile)
    if odd:
        return jnp.where(low, other, zero), jnp.where(low, zero, tile)
    return jnp.where(low, tile, zero), jnp.where(low, zero, other)


def attend_chunk(q_s, k_tiles, v_tiles, acc, masked, tok0, key0):
    keys_here = k_tiles(0).shape[0]
    tokens = q_s.shape[1] // PAIRS
    low = lax.broadcasted_iota(jnp.int32, (keys_here, LANES), 1) < HD
    one_lo = jnp.where(low, 1.0, 0.0).astype(jnp.bfloat16)
    one_hi = jnp.where(low, 0.0, 1.0).astype(jnp.bfloat16)
    for h in range(KV):
        k_lo, k_hi = paired(k_tiles(h // 2), h % 2)
        v_lo, v_hi = paired(v_tiles(h // 2), h % 2)
        kb = jnp.concatenate([k_lo, k_hi], 0).astype(jnp.bfloat16)
        vb = jnp.concatenate(
            [
                jnp.concatenate([v_lo.astype(jnp.bfloat16), one_lo], 1),
                jnp.concatenate([v_hi.astype(jnp.bfloat16), one_hi], 1),
            ],
            0,
        )
        s = lax.dot_general(
            q_s[h], kb, (((1,), (1,)), ((), ())), preferred_element_type=jnp.float32
        )
        if masked:
            tok = tok0 + lax.broadcasted_iota(jnp.int32, s.shape, 0) % tokens
            key = key0 + lax.broadcasted_iota(jnp.int32, s.shape, 1) % keys_here
            s = jnp.where(key <= tok, s, 0.0)
        w = (s * s).astype(jnp.bfloat16)
        acc[h] += jnp.dot(w, vb, preferred_element_type=jnp.float32)


def kernel(me_ref, q_ref, k_ref, v_ref, o_ref, q_s, acc):
    tokens = q_ref.shape[0]
    chunk = k_ref.shape[0]
    step = pl.program_id(0)
    tok0 = me_ref[0] * tokens
    last = tok0 // chunk

    @pl.when(step == 0)
    def _():
        for h in range(KV):
            for p in range(PAIRS):
                q_s[h, p * tokens : (p + 1) * tokens, :] = (
                    q_ref[:, (h * PAIRS + p) * LANES : (h * PAIRS + p + 1) * LANES].astype(
                        jnp.float32
                    )
                    * 0.125
                ).astype(jnp.bfloat16)
        acc[...] = jnp.zeros_like(acc)

    def k_tiles(i):
        return k_ref[:, i * LANES : (i + 1) * LANES]

    def v_tiles(i):
        return v_ref[:, i * LANES : (i + 1) * LANES]

    @pl.when(step < last)
    def _():
        attend_chunk(q_s, k_tiles, v_tiles, acc, False, 0, 0)

    @pl.when(step == last)
    def _():
        attend_chunk(q_s, k_tiles, v_tiles, acc, True, tok0, last * chunk)
        for h in range(KV):
            for p in range(PAIRS):
                part = acc[h, p * tokens : (p + 1) * tokens, :]
                o_ref[:, (h * PAIRS + p) * LANES : (h * PAIRS + p + 1) * LANES] = (
                    part[:, :LANES] / jnp.maximum(part[:, LANES:], 1.0)
                ).astype(jnp.bfloat16)


def on_device(queries, keys, values):
    axes = ("row", "col")
    tokens = queries.shape[0]
    me = (lax.axis_index("row") * lax.axis_size("col") + lax.axis_index("col")).reshape(1)
    both = jnp.concatenate([keys, values], 1).astype(jnp.float32)
    every = lax.all_gather(both, axes, axis=0, tiled=True)
    total = every.shape[0]
    chunk = 4 * tokens
    width = KV * HD
    return pl.pallas_call(
        kernel,
        out_shape=jax.ShapeDtypeStruct(queries.shape, jnp.bfloat16),
        grid_spec=pltpu.PrefetchScalarGridSpec(
            num_scalar_prefetch=1,
            grid=(total // chunk,),
            in_specs=[
                pl.BlockSpec(queries.shape, lambda s, m: (0, 0)),
                pl.BlockSpec((chunk, width), lambda s, m: (jnp.minimum(s, m[0] // 4), 0)),
                pl.BlockSpec((chunk, width), lambda s, m: (jnp.minimum(s, m[0] // 4), 1)),
            ],
            out_specs=pl.BlockSpec(queries.shape, lambda s, m: (0, 0)),
            scratch_shapes=[
                pltpu.VMEM((KV, PAIRS * tokens, LANES), jnp.bfloat16),
                pltpu.VMEM((KV, PAIRS * tokens, 2 * LANES), jnp.float32),
            ],
        ),
        compiler_params=pltpu.CompilerParams(vmem_limit_bytes=40 * 2**20),
    )(me, queries, every, every)


def solution(mesh):
    placed = P(("row", "col"), None)
    return jax.shard_map(
        on_device, mesh=mesh, in_specs=(placed,) * 3, out_specs=placed, check_vma=False
    )
```

```python
import functools

import jax
import jax.numpy as jnp
from jax import lax
from jax.experimental import pallas as pl
from jax.experimental.pallas import tpu as pltpu
from jax.sharding import PartitionSpec as P

HD = 64
KV = 4
QH = 32
PAIRS = QH // KV // 2
LANES = 2 * HD


def paired(tile, odd):
    low = lax.broadcasted_iota(jnp.int32, tile.shape, 1) < HD
    other = pltpu.roll(tile, HD, 1)
    zero = jnp.zeros_like(tile)
    if odd:
        return jnp.where(low, other, zero), jnp.where(low, zero, tile)
    return jnp.where(low, tile, zero), jnp.where(low, zero, other)


def attend_chunk(q_s, k_tiles, v_tiles, acc, masked, tok0, key0):
    keys_here = k_tiles(0).shape[0]
    tokens = q_s.shape[1] // PAIRS
    low = lax.broadcasted_iota(jnp.int32, (keys_here, LANES), 1) < HD
    one_lo = jnp.where(low, 1.0, 0.0).astype(jnp.bfloat16)
    one_hi = jnp.where(low, 0.0, 1.0).astype(jnp.bfloat16)
    for h in range(KV):
        k_lo, k_hi = paired(k_tiles(h // 2), h % 2)
        v_lo, v_hi = paired(v_tiles(h // 2), h % 2)
        kb = jnp.concatenate([k_lo, k_hi], 0).astype(jnp.bfloat16)
        vb = jnp.concatenate(
            [
                jnp.concatenate([v_lo.astype(jnp.bfloat16), one_lo], 1),
                jnp.concatenate([v_hi.astype(jnp.bfloat16), one_hi], 1),
            ],
            0,
        )
        s = lax.dot_general(
            q_s[h], kb, (((1,), (1,)), ((), ())), preferred_element_type=jnp.float32
        )
        if masked:
            tok = tok0 + lax.broadcasted_iota(jnp.int32, s.shape, 0) % tokens
            key = key0 + lax.broadcasted_iota(jnp.int32, s.shape, 1) % keys_here
            s = jnp.where(key <= tok, s, 0.0)
        w = (s * s).astype(jnp.bfloat16)
        acc[h] += jnp.dot(w, vb, preferred_element_type=jnp.float32)


def kernel(me_ref, q_ref, k_ref, v_ref, o_ref, q_s, acc):
    tokens = q_ref.shape[0]
    chunk = k_ref.shape[0]
    step = pl.program_id(0)
    tok0 = me_ref[0] * tokens
    last = tok0 // chunk

    @pl.when(step == 0)
    def _():
        for h in range(KV):
            for p in range(PAIRS):
                q_s[h, p * tokens : (p + 1) * tokens, :] = (
                    q_ref[:, (h * PAIRS + p) * LANES : (h * PAIRS + p + 1) * LANES].astype(
                        jnp.float32
                    )
                    * 0.125
                ).astype(jnp.bfloat16)
        acc[...] = jnp.zeros_like(acc)

    def k_tiles(i):
        return k_ref[:, i * LANES : (i + 1) * LANES]

    def v_tiles(i):
        return v_ref[:, i * LANES : (i + 1) * LANES]

    @pl.when(step < last)
    def _():
        attend_chunk(q_s, k_tiles, v_tiles, acc, False, 0, 0)

    @pl.when(step == last)
    def _():
        attend_chunk(q_s, k_tiles, v_tiles, acc, True, tok0, last * chunk)
        for h in range(KV):
            for p in range(PAIRS):
                part = acc[h, p * tokens : (p + 1) * tokens, :]
                o_ref[:, (h * PAIRS + p) * LANES : (h * PAIRS + p + 1) * LANES] = (
                    part[:, :LANES] / jnp.maximum(part[:, LANES:], 1.0)
                ).astype(jnp.bfloat16)


def on_device(queries, keys, values):
    axes = ("row", "col")
    tokens = queries.shape[0]
    me = (lax.axis_index("row") * lax.axis_size("col") + lax.axis_index("col")).reshape(1)
    both = jnp.concatenate([keys, values], 1).astype(jnp.float32)
    every = lax.all_gather(both, axes, axis=0, tiled=True)
    total = every.shape[0]
    chunk = 4 * tokens
    width = KV * HD
    return pl.pallas_call(
        kernel,
        out_shape=jax.ShapeDtypeStruct(queries.shape, jnp.bfloat16),
        grid_spec=pltpu.PrefetchScalarGridSpec(
            num_scalar_prefetch=1,
            grid=(total // chunk,),
            in_specs=[
                pl.BlockSpec(queries.shape, lambda s, m: (0, 0)),
                pl.BlockSpec((chunk, width), lambda s, m: (jnp.minimum(s, m[0] // 4), 0)),
                pl.BlockSpec((chunk, width), lambda s, m: (jnp.minimum(s, m[0] // 4), 1)),
            ],
            out_specs=pl.BlockSpec(queries.shape, lambda s, m: (0, 0)),
            scratch_shapes=[
                pltpu.VMEM((KV, PAIRS * tokens, LANES), jnp.bfloat16),
                pltpu.VMEM((KV, PAIRS * tokens, 2 * LANES), jnp.float32),
            ],
        ),
        compiler_params=pltpu.CompilerParams(vmem_limit_bytes=40 * 2**20),
    )(me, queries, every, every)


def fused_kernel(axes, shape, q_ref, k_ref, v_ref, o_ref, q_s, acc, held, send, recv):
    rows, cols = shape
    levels = rows // 2
    tokens = q_ref.shape[0]
    width = k_ref.shape[1]
    row, col = lax.axis_index(axes[0]), lax.axis_index(axes[1])
    z, c = row // 2, row % 2
    x, y = col % 2, col // 2
    x_col = y * 2 + 1 - x
    y_col = (1 - y) * 2 + x
    d_col = 3 - col
    x_dev, y_dev = (row, x_col), (row, y_col)
    core_dev = (z * 2 + 1 - c, col)
    up_dev, down_dev = (row + 2, col), (row - 2, col)
    not_top = z < levels - 1

    barrier = pltpu.get_barrier_semaphore()

    def greet(dev):
        pl.semaphore_signal(barrier, inc=1, device_id=dev, device_id_type=pl.DeviceIdType.MESH)

    for dev in (x_dev, y_dev, core_dev):
        greet(dev)

    @pl.when(not_top)
    def _():
        greet(up_dev)

    @pl.when(z > 0)
    def _():
        greet(down_dev)

    me = row * cols + col
    held[me, 0] = k_ref[...].astype(jnp.float32)
    held[me, 1] = v_ref[...].astype(jnp.float32)

    pl.semaphore_wait(barrier, 3 + jnp.minimum(z, 1) + jnp.minimum(levels - 1 - z, 1))

    def block(level, core, column):
        return (2 * (z - level) + core) * cols + column

    def whole(level, kind, b, dev):
        return pltpu.make_async_remote_copy(
            src_ref=held.at[b],
            dst_ref=held.at[b],
            send_sem=send.at[level, kind],
            recv_sem=recv.at[b, 0],
            device_id=dev,
            device_id_type=pl.DeviceIdType.MESH,
        )

    def piece(level, kind, b, part, dev):
        return pltpu.make_async_remote_copy(
            src_ref=held.at[b, part],
            dst_ref=held.at[b, part],
            send_sem=send.at[level, kind],
            recv_sem=recv.at[b, part],
            device_id=dev,
            device_id_type=pl.DeviceIdType.MESH,
        )

    def up_copy(level):
        return whole(level, 0, block(level, c, col), up_dev)

    def across(level):
        own = block(level, c, col)
        return whole(level, 1, own, x_dev), whole(level, 2, own, y_dev)

    def corner(level):
        return (
            piece(level, 3, block(level, c, x_col), 0, y_dev),
            piece(level, 4, block(level, c, y_col), 1, x_dev),
        )

    def to_core(level, which):
        column = (col, x_col, y_col, d_col)[which]
        return whole(level, 5 + which, block(level, c, column), core_dev)

    def own_sends(level):
        for copy in across(level):
            copy.start()

        @pl.when(not_top)
        def _():
            up_copy(level).start()

        @pl.when((level > 0) | (c == 0))
        def _():
            to_core(level, 0).start()

    def chunk(r, masked):
        def k_tiles(i):
            t = held[pl.ds(r * cols, cols), 0, :, i * LANES : (i + 1) * LANES]
            return t.reshape(cols * tokens, LANES)

        def v_tiles(i):
            t = held[pl.ds(r * cols, cols), 1, :, i * LANES : (i + 1) * LANES]
            return t.reshape(cols * tokens, LANES)

        attend_chunk(q_s, k_tiles, v_tiles, acc, masked, col * tokens, 0)

    own_sends(0)
    for h in range(KV):
        for p in range(PAIRS):
            q_s[h, p * tokens : (p + 1) * tokens, :] = (
                q_ref[:, (h * PAIRS + p) * LANES : (h * PAIRS + p + 1) * LANES].astype(jnp.float32)
                * 0.125
            ).astype(jnp.bfloat16)
    acc[...] = jnp.zeros_like(acc)

    def lap(level, _):
        inside = level <= z

        @pl.when(inside)
        def _():
            own = block(level, c, col)
            whole(level, 1, block(level, c, x_col), x_dev).wait_recv()
            whole(level, 2, block(level, c, y_col), y_dev).wait_recv()
            for copy in corner(level):
                copy.start()

            @pl.when((level > 0) | (c == 0))
            def _():
                to_core(level, 1).start()
                to_core(level, 2).start()

        @pl.when(level < z)
        def _():
            whole(level + 1, 0, block(level + 1, c, col), down_dev).wait_recv()
            own_sends(level + 1)

        @pl.when((level > 1) | ((level == 1) & (c == 1)))
        def _():
            for column in range(cols):
                whole(level - 1, 5, block(level - 1, 1 - c, column), core_dev).wait_recv()
            chunk(2 * (z - level + 1) + 1 - c, False)

        @pl.when(inside)
        def _():
            b = block(level, c, d_col)
            piece(level, 3, b, 0, y_dev).wait_recv()
            piece(level, 4, b, 1, x_dev).wait_recv()

            @pl.when((level > 0) | (c == 0))
            def _():
                to_core(level, 3).start()

        @pl.when(level == 0)
        def _():
            chunk(row, True)

        @pl.when(inside & (level > 0))
        def _():
            chunk(2 * (z - level) + c, False)

        return 0

    lax.fori_loop(0, z + 2, lap, 0)

    for h in range(KV):
        for p in range(PAIRS):
            part = acc[h, p * tokens : (p + 1) * tokens, :]
            o_ref[:, (h * PAIRS + p) * LANES : (h * PAIRS + p + 1) * LANES] = (
                part[:, :LANES] / jnp.maximum(part[:, LANES:], 1.0)
            ).astype(jnp.bfloat16)

    def drain(level, _):
        for copy in across(level) + corner(level):
            copy.wait_send()

        @pl.when(not_top)
        def _():
            up_copy(level).wait_send()

        @pl.when((level > 0) | (c == 0))
        def _():
            for which in range(4):
                to_core(level, which).wait_send()

        return 0

    lax.fori_loop(0, z + 1, drain, 0)


def fused(shape, queries, keys, values):
    tokens, width = keys.shape
    rows, cols = shape
    in_vmem = pl.BlockSpec(memory_space=pltpu.VMEM)
    return pl.pallas_call(
        functools.partial(fused_kernel, ("row", "col"), shape),
        out_shape=jax.ShapeDtypeStruct(queries.shape, jnp.bfloat16),
        in_specs=[in_vmem] * 3,
        out_specs=in_vmem,
        scratch_shapes=[
            pltpu.VMEM((KV, PAIRS * tokens, LANES), jnp.bfloat16),
            pltpu.VMEM((KV, PAIRS * tokens, 2 * LANES), jnp.float32),
            pltpu.VMEM((rows * cols, 2, tokens, width), jnp.float32),
            pltpu.SemaphoreType.DMA((rows // 2, 9)),
            pltpu.SemaphoreType.DMA((rows * cols, 2)),
        ],
        compiler_params=pltpu.CompilerParams(
            collective_id=0, has_side_effects=True, vmem_limit_bytes=40 * 2**20
        ),
    )(queries, keys, values)


def solution(mesh):
    placed = P(("row", "col"), None)
    rows, cols = mesh.shape["row"], mesh.shape["col"]

    def whole(queries, keys, values):
        held_bytes = keys.size * 8
        if cols == 4 and rows % 2 == 0 and held_bytes <= 16 * 2**20:
            local = functools.partial(fused, (rows, cols))
        else:
            local = on_device
        return jax.shard_map(
            local, mesh=mesh, in_specs=(placed,) * 3, out_specs=placed, check_vma=False
        )(queries, keys, values)

    return whole
```

```python
import functools

import jax
import jax.numpy as jnp
from jax import lax
from jax.experimental import pallas as pl
from jax.experimental.pallas import tpu as pltpu
from jax.sharding import PartitionSpec as P

HD = 64
KV = 4
QH = 32
PAIRS = QH // KV // 2
LANES = 2 * HD


def paired(tile, odd):
    low = lax.broadcasted_iota(jnp.int32, tile.shape, 1) < HD
    other = pltpu.roll(tile, HD, 1)
    zero = jnp.zeros_like(tile)
    if odd:
        return jnp.where(low, other, zero), jnp.where(low, zero, tile)
    return jnp.where(low, tile, zero), jnp.where(low, zero, other)


def attend_chunk(q_s, k_tiles, v_tiles, acc, masked, tok0, key0):
    keys_here = k_tiles(0).shape[0]
    tokens = q_s.shape[1] // PAIRS
    low = lax.broadcasted_iota(jnp.int32, (keys_here, LANES), 1) < HD
    one_lo = jnp.where(low, 1.0, 0.0).astype(jnp.bfloat16)
    one_hi = jnp.where(low, 0.0, 1.0).astype(jnp.bfloat16)
    for h in range(KV):
        k_lo, k_hi = paired(k_tiles(h // 2), h % 2)
        v_lo, v_hi = paired(v_tiles(h // 2), h % 2)
        kb = jnp.concatenate([k_lo, k_hi], 0).astype(jnp.bfloat16)
        vb = jnp.concatenate(
            [
                jnp.concatenate([v_lo.astype(jnp.bfloat16), one_lo], 1),
                jnp.concatenate([v_hi.astype(jnp.bfloat16), one_hi], 1),
            ],
            0,
        )
        s = lax.dot_general(
            q_s[h], kb, (((1,), (1,)), ((), ())), preferred_element_type=jnp.float32
        )
        if masked:
            tok = tok0 + lax.broadcasted_iota(jnp.int32, s.shape, 0) % tokens
            key = key0 + lax.broadcasted_iota(jnp.int32, s.shape, 1) % keys_here
            s = jnp.where(key <= tok, s, 0.0)
        w = (s * s).astype(jnp.bfloat16)
        acc[h] += jnp.dot(w, vb, preferred_element_type=jnp.float32)


def kernel(me_ref, q_ref, k_ref, v_ref, o_ref, q_s, acc):
    tokens = q_ref.shape[0]
    chunk = k_ref.shape[0]
    step = pl.program_id(0)
    tok0 = me_ref[0] * tokens
    last = tok0 // chunk

    @pl.when(step == 0)
    def _():
        for h in range(KV):
            for p in range(PAIRS):
                q_s[h, p * tokens : (p + 1) * tokens, :] = (
                    q_ref[:, (h * PAIRS + p) * LANES : (h * PAIRS + p + 1) * LANES].astype(
                        jnp.float32
                    )
                    * 0.125
                ).astype(jnp.bfloat16)
        acc[...] = jnp.zeros_like(acc)

    def k_tiles(i):
        return k_ref[:, i * LANES : (i + 1) * LANES]

    def v_tiles(i):
        return v_ref[:, i * LANES : (i + 1) * LANES]

    @pl.when(step < last)
    def _():
        attend_chunk(q_s, k_tiles, v_tiles, acc, False, 0, 0)

    @pl.when(step == last)
    def _():
        attend_chunk(q_s, k_tiles, v_tiles, acc, True, tok0, last * chunk)
        for h in range(KV):
            for p in range(PAIRS):
                part = acc[h, p * tokens : (p + 1) * tokens, :]
                o_ref[:, (h * PAIRS + p) * LANES : (h * PAIRS + p + 1) * LANES] = (
                    part[:, :LANES] / jnp.maximum(part[:, LANES:], 1.0)
                ).astype(jnp.bfloat16)


def on_device(queries, keys, values):
    axes = ("row", "col")
    tokens = queries.shape[0]
    me = (lax.axis_index("row") * lax.axis_size("col") + lax.axis_index("col")).reshape(1)
    both = jnp.concatenate([keys, values], 1).astype(jnp.float32)
    every = lax.all_gather(both, axes, axis=0, tiled=True)
    total = every.shape[0]
    chunk = 4 * tokens
    width = KV * HD
    return pl.pallas_call(
        kernel,
        out_shape=jax.ShapeDtypeStruct(queries.shape, jnp.bfloat16),
        grid_spec=pltpu.PrefetchScalarGridSpec(
            num_scalar_prefetch=1,
            grid=(total // chunk,),
            in_specs=[
                pl.BlockSpec(queries.shape, lambda s, m: (0, 0)),
                pl.BlockSpec((chunk, width), lambda s, m: (jnp.minimum(s, m[0] // 4), 0)),
                pl.BlockSpec((chunk, width), lambda s, m: (jnp.minimum(s, m[0] // 4), 1)),
            ],
            out_specs=pl.BlockSpec(queries.shape, lambda s, m: (0, 0)),
            scratch_shapes=[
                pltpu.VMEM((KV, PAIRS * tokens, LANES), jnp.bfloat16),
                pltpu.VMEM((KV, PAIRS * tokens, 2 * LANES), jnp.float32),
            ],
        ),
        compiler_params=pltpu.CompilerParams(vmem_limit_bytes=40 * 2**20),
    )(me, queries, every, every)


def fused_kernel(
    axes, shape, q_hbm, k_hbm, v_hbm, o_ref, q_ref, k_ref, v_ref, q_s, acc, held, local, send, recv
):
    rows, cols = shape
    levels = rows // 2
    tokens = q_ref.shape[0]
    width = k_ref.shape[1]
    row, col = lax.axis_index(axes[0]), lax.axis_index(axes[1])
    z, c = row // 2, row % 2
    x, y = col % 2, col // 2
    x_col = y * 2 + 1 - x
    y_col = (1 - y) * 2 + x
    d_col = 3 - col
    x_dev, y_dev = (row, x_col), (row, y_col)
    core_dev = (z * 2 + 1 - c, col)
    up_dev, down_dev = (row + 2, col), (row - 2, col)
    not_top = z < levels - 1

    loads = [
        pltpu.make_async_copy(src, dst, local.at[i])
        for i, (src, dst) in enumerate(((k_hbm, k_ref), (v_hbm, v_ref), (q_hbm, q_ref)))
    ]
    for load in loads:
        load.start()
    barrier = pltpu.get_barrier_semaphore()

    def greet(dev):
        pl.semaphore_signal(barrier, inc=1, device_id=dev, device_id_type=pl.DeviceIdType.MESH)

    for dev in (x_dev, y_dev, core_dev):
        greet(dev)

    @pl.when(not_top)
    def _():
        greet(up_dev)

    @pl.when(z > 0)
    def _():
        greet(down_dev)

    me = row * cols + col
    loads[0].wait()
    loads[1].wait()
    held[me, 0] = k_ref[...].astype(jnp.float32)
    held[me, 1] = v_ref[...].astype(jnp.float32)

    pl.semaphore_wait(barrier, 3 + jnp.minimum(z, 1) + jnp.minimum(levels - 1 - z, 1))

    def block(level, core, column):
        return (2 * (z - level) + core) * cols + column

    def whole(level, kind, b, dev):
        return pltpu.make_async_remote_copy(
            src_ref=held.at[b],
            dst_ref=held.at[b],
            send_sem=send.at[level, kind],
            recv_sem=recv.at[b, 0],
            device_id=dev,
            device_id_type=pl.DeviceIdType.MESH,
        )

    def piece(level, kind, b, part, dev):
        return pltpu.make_async_remote_copy(
            src_ref=held.at[b, part],
            dst_ref=held.at[b, part],
            send_sem=send.at[level, kind],
            recv_sem=recv.at[b, part],
            device_id=dev,
            device_id_type=pl.DeviceIdType.MESH,
        )

    def up_copy(level):
        return whole(level, 0, block(level, c, col), up_dev)

    def across(level):
        own = block(level, c, col)
        return whole(level, 1, own, x_dev), whole(level, 2, own, y_dev)

    def corner(level):
        return (
            piece(level, 3, block(level, c, x_col), 0, y_dev),
            piece(level, 4, block(level, c, y_col), 1, x_dev),
        )

    def to_core(level, which):
        column = (col, x_col, y_col, d_col)[which]
        return whole(level, 5 + which, block(level, c, column), core_dev)

    def own_sends(level):
        for copy in across(level):
            copy.start()

        @pl.when(not_top)
        def _():
            up_copy(level).start()

        @pl.when((level > 0) | (c == 0))
        def _():
            to_core(level, 0).start()

    def chunk(first, second, masked):
        def tiles(part, i):
            lanes = slice(i * LANES, (i + 1) * LANES)
            halves = [
                held[pl.ds(b, 2), part, :, lanes].reshape(2 * tokens, LANES)
                for b in (first, second)
            ]
            return jnp.concatenate(halves, 0)

        attend_chunk(
            q_s,
            lambda i: tiles(0, i),
            lambda i: tiles(1, i),
            acc,
            masked,
            col * tokens,
            0,
        )

    def core_arrival(level, column):
        whole(level, 5, block(level, 1 - c, column), core_dev).wait_recv()

    def from_below(level):
        whole(level, 0, block(level, c, col), down_dev).wait_recv()
        own_sends(level)

    own_sends(0)
    loads[2].wait()
    for h in range(KV):
        for p in range(PAIRS):
            q_s[h, p * tokens : (p + 1) * tokens, :] = (
                q_ref[:, (h * PAIRS + p) * LANES : (h * PAIRS + p + 1) * LANES].astype(jnp.float32)
                * 0.125
            ).astype(jnp.bfloat16)
    acc[...] = jnp.zeros_like(acc)

    def lap(level, _):
        inside = level <= z

        @pl.when(inside)
        def _():
            whole(level, 1, block(level, c, x_col), x_dev).wait_recv()
            whole(level, 2, block(level, c, y_col), y_dev).wait_recv()
            for copy in corner(level):
                copy.start()

            @pl.when((level > 0) | (c == 0))
            def _():
                to_core(level, 1).start()
                to_core(level, 2).start()

        @pl.when((level == 0) & (z > 0))
        def _():
            from_below(1)

        @pl.when((level > 1) | ((level == 1) & (c == 1)))
        def _():
            core_arrival(level - 1, y_col)
            core_arrival(level - 1, d_col)

            @pl.when(level == 1)
            def _():
                core_arrival(0, col)
                core_arrival(0, x_col)

            far = 2 * (1 - y)
            first = jnp.where(level == 1, block(0, 1 - c, 0), block(level - 1, c, far))
            second = jnp.where(level == 1, block(0, 1 - c, 2), block(level - 1, 1 - c, far))
            chunk(first, second, False)

        @pl.when(inside)
        def _():
            b = block(level, c, d_col)
            piece(level, 3, b, 0, y_dev).wait_recv()
            piece(level, 4, b, 1, x_dev).wait_recv()

            @pl.when((level > 0) | (c == 0))
            def _():
                to_core(level, 3).start()

        @pl.when(level == 0)
        def _():
            chunk(row * cols, row * cols + 2, True)

        @pl.when(inside & (level > 0))
        def _():
            core_arrival(level, col)
            core_arrival(level, x_col)
            chunk(block(level, c, 2 * y), block(level, 1 - c, 2 * y), False)

        @pl.when(level + 2 <= z)
        def _():
            from_below(level + 2)

        return 0

    lax.fori_loop(0, z + 2, lap, 0)

    for h in range(KV):
        for p in range(PAIRS):
            part = acc[h, p * tokens : (p + 1) * tokens, :]
            o_ref[:, (h * PAIRS + p) * LANES : (h * PAIRS + p + 1) * LANES] = (
                part[:, :LANES] / jnp.maximum(part[:, LANES:], 1.0)
            ).astype(jnp.bfloat16)

    def drain(level, _):
        for copy in across(level) + corner(level):
            copy.wait_send()

        @pl.when(not_top)
        def _():
            up_copy(level).wait_send()

        @pl.when((level > 0) | (c == 0))
        def _():
            for which in range(4):
                to_core(level, which).wait_send()

        return 0

    lax.fori_loop(0, z + 1, drain, 0)


def fused(shape, queries, keys, values):
    tokens, width = keys.shape
    rows, cols = shape
    in_vmem = pl.BlockSpec(memory_space=pltpu.VMEM)
    return pl.pallas_call(
        functools.partial(fused_kernel, ("row", "col"), shape),
        out_shape=jax.ShapeDtypeStruct(queries.shape, jnp.bfloat16),
        in_specs=[pl.BlockSpec(memory_space=pltpu.HBM)] * 3,
        out_specs=in_vmem,
        scratch_shapes=[
            pltpu.VMEM(queries.shape, jnp.bfloat16),
            pltpu.VMEM(keys.shape, jnp.bfloat16),
            pltpu.VMEM(values.shape, jnp.bfloat16),
            pltpu.VMEM((KV, PAIRS * tokens, LANES), jnp.bfloat16),
            pltpu.VMEM((KV, PAIRS * tokens, 2 * LANES), jnp.float32),
            pltpu.VMEM((rows * cols, 2, tokens, width), jnp.float32),
            pltpu.SemaphoreType.DMA((3,)),
            pltpu.SemaphoreType.DMA((rows // 2, 9)),
            pltpu.SemaphoreType.DMA((rows * cols, 2)),
        ],
        compiler_params=pltpu.CompilerParams(
            collective_id=0, has_side_effects=True, vmem_limit_bytes=60 * 2**20
        ),
    )(queries, keys, values)


def solution(mesh):
    placed = P(("row", "col"), None)
    rows, cols = mesh.shape["row"], mesh.shape["col"]

    def whole(queries, keys, values):
        held_bytes = keys.size * 8
        if cols == 4 and rows % 2 == 0 and held_bytes <= 16 * 2**20:
            local = functools.partial(fused, (rows, cols))
        else:
            local = on_device
        return jax.shard_map(
            local, mesh=mesh, in_specs=(placed,) * 3, out_specs=placed, check_vma=False
        )(queries, keys, values)

    return whole
```

```python
import functools

import jax
import jax.numpy as jnp
from jax import lax
from jax.experimental import pallas as pl
from jax.experimental.pallas import tpu as pltpu
from jax.sharding import PartitionSpec as P

HD = 64
KV = 4
QH = 32
PAIRS = QH // KV // 2
LANES = 2 * HD


def paired(tile, odd):
    low = lax.broadcasted_iota(jnp.int32, tile.shape, 1) < HD
    other = pltpu.roll(tile, HD, 1)
    zero = jnp.zeros_like(tile)
    if odd:
        return jnp.where(low, other, zero), jnp.where(low, zero, tile)
    return jnp.where(low, tile, zero), jnp.where(low, zero, other)


def attend_chunk(q_s, k_tiles, v_tiles, acc, masked, tok0, key0):
    keys_here = k_tiles(0).shape[0]
    tokens = q_s.shape[1] // PAIRS
    low = lax.broadcasted_iota(jnp.int32, (keys_here, LANES), 1) < HD
    one_lo = jnp.where(low, 1.0, 0.0).astype(jnp.bfloat16)
    one_hi = jnp.where(low, 0.0, 1.0).astype(jnp.bfloat16)
    for h in range(KV):
        k_lo, k_hi = paired(k_tiles(h // 2), h % 2)
        v_lo, v_hi = paired(v_tiles(h // 2), h % 2)
        kb = jnp.concatenate([k_lo, k_hi], 0).astype(jnp.bfloat16)
        vb = jnp.concatenate(
            [
                jnp.concatenate([v_lo.astype(jnp.bfloat16), one_lo], 1),
                jnp.concatenate([v_hi.astype(jnp.bfloat16), one_hi], 1),
            ],
            0,
        )
        s = lax.dot_general(
            q_s[h], kb, (((1,), (1,)), ((), ())), preferred_element_type=jnp.float32
        )
        if masked:
            tok = tok0 + lax.broadcasted_iota(jnp.int32, s.shape, 0) % tokens
            key = key0 + lax.broadcasted_iota(jnp.int32, s.shape, 1) % keys_here
            s = jnp.where(key <= tok, s, 0.0)
        w = (s * s).astype(jnp.bfloat16)
        acc[h] += jnp.dot(w, vb, preferred_element_type=jnp.float32)


def kernel(me_ref, q_ref, k_ref, v_ref, o_ref, q_s, acc):
    tokens = q_ref.shape[0]
    chunk = k_ref.shape[0]
    step = pl.program_id(0)
    tok0 = me_ref[0] * tokens
    last = tok0 // chunk

    @pl.when(step == 0)
    def _():
        for h in range(KV):
            for p in range(PAIRS):
                q_s[h, p * tokens : (p + 1) * tokens, :] = (
                    q_ref[:, (h * PAIRS + p) * LANES : (h * PAIRS + p + 1) * LANES].astype(
                        jnp.float32
                    )
                    * 0.125
                ).astype(jnp.bfloat16)
        acc[...] = jnp.zeros_like(acc)

    def k_tiles(i):
        return k_ref[:, i * LANES : (i + 1) * LANES]

    def v_tiles(i):
        return v_ref[:, i * LANES : (i + 1) * LANES]

    @pl.when(step < last)
    def _():
        attend_chunk(q_s, k_tiles, v_tiles, acc, False, 0, 0)

    @pl.when(step == last)
    def _():
        attend_chunk(q_s, k_tiles, v_tiles, acc, True, tok0, last * chunk)
        for h in range(KV):
            for p in range(PAIRS):
                part = acc[h, p * tokens : (p + 1) * tokens, :]
                o_ref[:, (h * PAIRS + p) * LANES : (h * PAIRS + p + 1) * LANES] = (
                    part[:, :LANES] / jnp.maximum(part[:, LANES:], 1.0)
                ).astype(jnp.bfloat16)


def on_device(queries, keys, values):
    axes = ("row", "col")
    tokens = queries.shape[0]
    me = (lax.axis_index("row") * lax.axis_size("col") + lax.axis_index("col")).reshape(1)
    both = jnp.concatenate([keys, values], 1).astype(jnp.float32)
    every = lax.all_gather(both, axes, axis=0, tiled=True)
    total = every.shape[0]
    chunk = 4 * tokens
    width = KV * HD
    return pl.pallas_call(
        kernel,
        out_shape=jax.ShapeDtypeStruct(queries.shape, jnp.bfloat16),
        grid_spec=pltpu.PrefetchScalarGridSpec(
            num_scalar_prefetch=1,
            grid=(total // chunk,),
            in_specs=[
                pl.BlockSpec(queries.shape, lambda s, m: (0, 0)),
                pl.BlockSpec((chunk, width), lambda s, m: (jnp.minimum(s, m[0] // 4), 0)),
                pl.BlockSpec((chunk, width), lambda s, m: (jnp.minimum(s, m[0] // 4), 1)),
            ],
            out_specs=pl.BlockSpec(queries.shape, lambda s, m: (0, 0)),
            scratch_shapes=[
                pltpu.VMEM((KV, PAIRS * tokens, LANES), jnp.bfloat16),
                pltpu.VMEM((KV, PAIRS * tokens, 2 * LANES), jnp.float32),
            ],
        ),
        compiler_params=pltpu.CompilerParams(vmem_limit_bytes=40 * 2**20),
    )(me, queries, every, every)


def fused_kernel(
    axes, shape, q_hbm, k_hbm, v_hbm, o_ref, q_ref, k_ref, v_ref, q_s, acc, held, local, send, recv
):
    rows, cols = shape
    levels = rows // 2
    tokens = q_ref.shape[0]
    width = k_ref.shape[1]
    row, col = lax.axis_index(axes[0]), lax.axis_index(axes[1])
    z, c = row // 2, row % 2
    x, y = col % 2, col // 2
    x_col = y * 2 + 1 - x
    y_col = (1 - y) * 2 + x
    d_col = 3 - col
    x_dev, y_dev = (row, x_col), (row, y_col)
    core_dev = (z * 2 + 1 - c, col)
    up_dev, down_dev = (row + 2, col), (row - 2, col)
    not_top = z < levels - 1

    loads = [
        pltpu.make_async_copy(src, dst, local.at[i])
        for i, (src, dst) in enumerate(((k_hbm, k_ref), (v_hbm, v_ref), (q_hbm, q_ref)))
    ]
    for load in loads:
        load.start()
    barrier = pltpu.get_barrier_semaphore()

    def greet(dev):
        pl.semaphore_signal(barrier, inc=1, device_id=dev, device_id_type=pl.DeviceIdType.MESH)

    for dev in (x_dev, y_dev, core_dev):
        greet(dev)

    @pl.when(not_top)
    def _():
        greet(up_dev)

    @pl.when(z > 0)
    def _():
        greet(down_dev)

    me = row * cols + col
    loads[0].wait()
    loads[1].wait()
    held[me, 0] = k_ref[...].astype(jnp.float32)
    held[me, 1] = v_ref[...].astype(jnp.float32)

    pl.semaphore_wait(barrier, 3 + jnp.minimum(z, 1) + jnp.minimum(levels - 1 - z, 1))

    def block(level, core, column):
        return (2 * (z - level) + core) * cols + column

    def whole(level, kind, b, dev):
        return pltpu.make_async_remote_copy(
            src_ref=held.at[b],
            dst_ref=held.at[b],
            send_sem=send.at[level, kind],
            recv_sem=recv.at[b, 0],
            device_id=dev,
            device_id_type=pl.DeviceIdType.MESH,
        )

    def piece(level, kind, b, part, dev):
        return pltpu.make_async_remote_copy(
            src_ref=held.at[b, part],
            dst_ref=held.at[b, part],
            send_sem=send.at[level, kind],
            recv_sem=recv.at[b, part],
            device_id=dev,
            device_id_type=pl.DeviceIdType.MESH,
        )

    def up_copy(level):
        return whole(level, 0, block(level, c, col), up_dev)

    def across(level):
        own = block(level, c, col)
        return (
            piece(level, 1, own, 0, x_dev),
            piece(level, 2, own, 1, y_dev),
            piece(level, 9, own, 1, x_dev),
            piece(level, 10, own, 0, y_dev),
        )

    def corner(level):
        return (
            piece(level, 3, block(level, c, x_col), 0, y_dev),
            piece(level, 4, block(level, c, y_col), 1, x_dev),
        )

    def to_core(level, which):
        column = (col, x_col, y_col, d_col)[which]
        return whole(level, 5 + which, block(level, c, column), core_dev)

    def own_sends(level):
        for copy in across(level):
            copy.start()

        @pl.when(not_top)
        def _():
            up_copy(level).start()

        @pl.when((level > 0) | (c == 0))
        def _():
            to_core(level, 0).start()

    def chunk(first, second, masked):
        def tiles(part, i):
            lanes = slice(i * LANES, (i + 1) * LANES)
            halves = [
                held[pl.ds(b, 2), part, :, lanes].reshape(2 * tokens, LANES)
                for b in (first, second)
            ]
            return jnp.concatenate(halves, 0)

        attend_chunk(
            q_s,
            lambda i: tiles(0, i),
            lambda i: tiles(1, i),
            acc,
            masked,
            col * tokens,
            0,
        )

    def core_arrival(level, column):
        whole(level, 5, block(level, 1 - c, column), core_dev).wait_recv()

    def from_below(level):
        whole(level, 0, block(level, c, col), down_dev).wait_recv()
        own_sends(level)

    own_sends(0)
    loads[2].wait()
    for h in range(KV):
        for p in range(PAIRS):
            q_s[h, p * tokens : (p + 1) * tokens, :] = (
                q_ref[:, (h * PAIRS + p) * LANES : (h * PAIRS + p + 1) * LANES].astype(jnp.float32)
                * 0.125
            ).astype(jnp.bfloat16)
    acc[...] = jnp.zeros_like(acc)

    def lap(level, _):
        inside = level <= z

        @pl.when(inside)
        def _():
            piece(level, 1, block(level, c, x_col), 0, x_dev).wait_recv()
            piece(level, 2, block(level, c, y_col), 1, y_dev).wait_recv()
            for copy in corner(level):
                copy.start()

        @pl.when(level < z)
        def _():
            from_below(level + 1)

        @pl.when((level > 1) | ((level == 1) & (c == 1)))
        def _():
            core_arrival(level - 1, y_col)
            core_arrival(level - 1, d_col)

            @pl.when(level == 1)
            def _():
                core_arrival(0, col)
                core_arrival(0, x_col)

            far = 2 * (1 - y)
            first = jnp.where(level == 1, block(0, 1 - c, 0), block(level - 1, c, far))
            second = jnp.where(level == 1, block(0, 1 - c, 2), block(level - 1, 1 - c, far))
            chunk(first, second, False)

        @pl.when(inside)
        def _():
            piece(level, 9, block(level, c, x_col), 1, x_dev).wait_recv()
            piece(level, 10, block(level, c, y_col), 0, y_dev).wait_recv()

            @pl.when((level > 0) | (c == 0))
            def _():
                to_core(level, 1).start()
                to_core(level, 2).start()

        @pl.when(inside & (level > 0))
        def _():
            core_arrival(level, col)
            core_arrival(level, x_col)
            chunk(block(level, c, 2 * y), block(level, 1 - c, 2 * y), False)

        @pl.when(inside)
        def _():
            b = block(level, c, d_col)
            piece(level, 3, b, 0, y_dev).wait_recv()
            piece(level, 4, b, 1, x_dev).wait_recv()

            @pl.when((level > 0) | (c == 0))
            def _():
                to_core(level, 3).start()

        @pl.when(level == 0)
        def _():
            chunk(row * cols, row * cols + 2, True)

        return 0

    lax.fori_loop(0, z + 2, lap, 0)

    for h in range(KV):
        for p in range(PAIRS):
            part = acc[h, p * tokens : (p + 1) * tokens, :]
            o_ref[:, (h * PAIRS + p) * LANES : (h * PAIRS + p + 1) * LANES] = (
                part[:, :LANES] / jnp.maximum(part[:, LANES:], 1.0)
            ).astype(jnp.bfloat16)

    def drain(level, _):
        for copy in across(level) + corner(level):
            copy.wait_send()

        @pl.when(not_top)
        def _():
            up_copy(level).wait_send()

        @pl.when((level > 0) | (c == 0))
        def _():
            for which in range(4):
                to_core(level, which).wait_send()

        return 0

    lax.fori_loop(0, z + 1, drain, 0)


def fused(shape, queries, keys, values):
    tokens, width = keys.shape
    rows, cols = shape
    in_vmem = pl.BlockSpec(memory_space=pltpu.VMEM)
    return pl.pallas_call(
        functools.partial(fused_kernel, ("row", "col"), shape),
        out_shape=jax.ShapeDtypeStruct(queries.shape, jnp.bfloat16),
        in_specs=[pl.BlockSpec(memory_space=pltpu.HBM)] * 3,
        out_specs=in_vmem,
        scratch_shapes=[
            pltpu.VMEM(queries.shape, jnp.bfloat16),
            pltpu.VMEM(keys.shape, jnp.bfloat16),
            pltpu.VMEM(values.shape, jnp.bfloat16),
            pltpu.VMEM((KV, PAIRS * tokens, LANES), jnp.bfloat16),
            pltpu.VMEM((KV, PAIRS * tokens, 2 * LANES), jnp.float32),
            pltpu.VMEM((rows * cols, 2, tokens, width), jnp.float32),
            pltpu.SemaphoreType.DMA((3,)),
            pltpu.SemaphoreType.DMA((rows // 2, 11)),
            pltpu.SemaphoreType.DMA((rows * cols, 2)),
        ],
        compiler_params=pltpu.CompilerParams(
            collective_id=0, has_side_effects=True, vmem_limit_bytes=60 * 2**20
        ),
    )(queries, keys, values)


def solution(mesh):
    placed = P(("row", "col"), None)
    rows, cols = mesh.shape["row"], mesh.shape["col"]

    def whole(queries, keys, values):
        held_bytes = keys.size * 8
        if cols == 4 and rows % 2 == 0 and held_bytes <= 16 * 2**20:
            local = functools.partial(fused, (rows, cols))
        else:
            local = on_device
        return jax.shard_map(
            local, mesh=mesh, in_specs=(placed,) * 3, out_specs=placed, check_vma=False
        )(queries, keys, values)

    return whole
```

```python
import functools

import jax
import jax.numpy as jnp
from jax import lax
from jax.experimental import pallas as pl
from jax.experimental.pallas import tpu as pltpu
from jax.sharding import PartitionSpec as P

HD = 64
KV = 4
QH = 32
PAIRS = QH // KV // 2
LANES = 2 * HD


def paired(tile, odd):
    low = lax.broadcasted_iota(jnp.int32, tile.shape, 1) < HD
    other = pltpu.roll(tile, HD, 1)
    zero = jnp.zeros_like(tile)
    if odd:
        return jnp.where(low, other, zero), jnp.where(low, zero, tile)
    return jnp.where(low, tile, zero), jnp.where(low, zero, other)


def attend_chunk(q_s, k_tiles, v_tiles, acc, masked, tok0, key0):
    keys_here = k_tiles(0).shape[0]
    tokens = q_s.shape[1] // PAIRS
    low = lax.broadcasted_iota(jnp.int32, (keys_here, LANES), 1) < HD
    one_lo = jnp.where(low, 1.0, 0.0).astype(jnp.bfloat16)
    one_hi = jnp.where(low, 0.0, 1.0).astype(jnp.bfloat16)
    for h in range(KV):
        k_lo, k_hi = paired(k_tiles(h // 2), h % 2)
        v_lo, v_hi = paired(v_tiles(h // 2), h % 2)
        kb = jnp.concatenate([k_lo, k_hi], 0).astype(jnp.bfloat16)
        vb = jnp.concatenate(
            [
                jnp.concatenate([v_lo.astype(jnp.bfloat16), one_lo], 1),
                jnp.concatenate([v_hi.astype(jnp.bfloat16), one_hi], 1),
            ],
            0,
        )
        s = lax.dot_general(
            q_s[h], kb, (((1,), (1,)), ((), ())), preferred_element_type=jnp.float32
        )
        if masked:
            tok = tok0 + lax.broadcasted_iota(jnp.int32, s.shape, 0) % tokens
            key = key0 + lax.broadcasted_iota(jnp.int32, s.shape, 1) % keys_here
            s = jnp.where(key <= tok, s, 0.0)
        w = (s * s).astype(jnp.bfloat16)
        acc[h] += jnp.dot(w, vb, preferred_element_type=jnp.float32)


def kernel(me_ref, q_ref, k_ref, v_ref, o_ref, q_s, acc):
    tokens = q_ref.shape[0]
    chunk = k_ref.shape[0]
    step = pl.program_id(0)
    tok0 = me_ref[0] * tokens
    last = tok0 // chunk

    @pl.when(step == 0)
    def _():
        for h in range(KV):
            for p in range(PAIRS):
                q_s[h, p * tokens : (p + 1) * tokens, :] = (
                    q_ref[:, (h * PAIRS + p) * LANES : (h * PAIRS + p + 1) * LANES].astype(
                        jnp.float32
                    )
                    * 0.125
                ).astype(jnp.bfloat16)
        acc[...] = jnp.zeros_like(acc)

    def k_tiles(i):
        return k_ref[:, i * LANES : (i + 1) * LANES]

    def v_tiles(i):
        return v_ref[:, i * LANES : (i + 1) * LANES]

    @pl.when(step < last)
    def _():
        attend_chunk(q_s, k_tiles, v_tiles, acc, False, 0, 0)

    @pl.when(step == last)
    def _():
        attend_chunk(q_s, k_tiles, v_tiles, acc, True, tok0, last * chunk)
        for h in range(KV):
            for p in range(PAIRS):
                part = acc[h, p * tokens : (p + 1) * tokens, :]
                o_ref[:, (h * PAIRS + p) * LANES : (h * PAIRS + p + 1) * LANES] = (
                    part[:, :LANES] / jnp.maximum(part[:, LANES:], 1.0)
                ).astype(jnp.bfloat16)


def on_device(queries, keys, values):
    axes = ("row", "col")
    tokens = queries.shape[0]
    me = (lax.axis_index("row") * lax.axis_size("col") + lax.axis_index("col")).reshape(1)
    both = jnp.concatenate([keys, values], 1).astype(jnp.float32)
    every = lax.all_gather(both, axes, axis=0, tiled=True)
    total = every.shape[0]
    chunk = 4 * tokens
    width = KV * HD
    return pl.pallas_call(
        kernel,
        out_shape=jax.ShapeDtypeStruct(queries.shape, jnp.bfloat16),
        grid_spec=pltpu.PrefetchScalarGridSpec(
            num_scalar_prefetch=1,
            grid=(total // chunk,),
            in_specs=[
                pl.BlockSpec(queries.shape, lambda s, m: (0, 0)),
                pl.BlockSpec((chunk, width), lambda s, m: (jnp.minimum(s, m[0] // 4), 0)),
                pl.BlockSpec((chunk, width), lambda s, m: (jnp.minimum(s, m[0] // 4), 1)),
            ],
            out_specs=pl.BlockSpec(queries.shape, lambda s, m: (0, 0)),
            scratch_shapes=[
                pltpu.VMEM((KV, PAIRS * tokens, LANES), jnp.bfloat16),
                pltpu.VMEM((KV, PAIRS * tokens, 2 * LANES), jnp.float32),
            ],
        ),
        compiler_params=pltpu.CompilerParams(vmem_limit_bytes=40 * 2**20),
    )(me, queries, every, every)


def fused_kernel(
    axes, shape, q_hbm, k_hbm, v_hbm, o_ref, q_ref, k_ref, v_ref, q_s, acc, held, local, send, recv
):
    rows, cols = shape
    levels = rows // 2
    tokens = q_ref.shape[0]
    width = k_ref.shape[1]
    row, col = lax.axis_index(axes[0]), lax.axis_index(axes[1])
    z, c = row // 2, row % 2
    x, y = col % 2, col // 2
    x_col = y * 2 + 1 - x
    y_col = (1 - y) * 2 + x
    d_col = 3 - col
    x_dev, y_dev = (row, x_col), (row, y_col)
    core_dev = (z * 2 + 1 - c, col)
    up_dev, down_dev = (row + 2, col), (row - 2, col)
    not_top = z < levels - 1

    loads = [
        pltpu.make_async_copy(src, dst, local.at[i])
        for i, (src, dst) in enumerate(((k_hbm, k_ref), (v_hbm, v_ref), (q_hbm, q_ref)))
    ]
    for load in loads:
        load.start()
    barrier = pltpu.get_barrier_semaphore()

    def greet(dev):
        pl.semaphore_signal(barrier, inc=1, device_id=dev, device_id_type=pl.DeviceIdType.MESH)

    for dev in (x_dev, y_dev, core_dev):
        greet(dev)

    @pl.when(not_top)
    def _():
        greet(up_dev)

    @pl.when(z > 0)
    def _():
        greet(down_dev)

    me = row * cols + col
    loads[0].wait()
    loads[1].wait()
    held[me, 0] = k_ref[...].astype(jnp.float32)
    held[me, 1] = v_ref[...].astype(jnp.float32)

    pl.semaphore_wait(barrier, 3 + jnp.minimum(z, 1) + jnp.minimum(levels - 1 - z, 1))

    def block(level, core, column):
        return (2 * (z - level) + core) * cols + column

    def whole(level, kind, b, dev):
        return pltpu.make_async_remote_copy(
            src_ref=held.at[b],
            dst_ref=held.at[b],
            send_sem=send.at[level, kind],
            recv_sem=recv.at[b, 0],
            device_id=dev,
            device_id_type=pl.DeviceIdType.MESH,
        )

    def piece(level, kind, b, part, dev):
        return pltpu.make_async_remote_copy(
            src_ref=held.at[b, part],
            dst_ref=held.at[b, part],
            send_sem=send.at[level, kind],
            recv_sem=recv.at[b, part],
            device_id=dev,
            device_id_type=pl.DeviceIdType.MESH,
        )

    def up_copy(level):
        return whole(level, 0, block(level, c, col), up_dev)

    def across(level):
        own = block(level, c, col)
        return (
            piece(level, 1, own, 0, x_dev),
            piece(level, 2, own, 1, y_dev),
            piece(level, 9, own, 1, x_dev),
            piece(level, 10, own, 0, y_dev),
        )

    def corner(level):
        return (
            piece(level, 3, block(level, c, x_col), 0, y_dev),
            piece(level, 4, block(level, c, y_col), 1, x_dev),
        )

    def to_core(level, which):
        column = (col, x_col, y_col, d_col)[which]
        return whole(level, 5 + which, block(level, c, column), core_dev)

    def own_sends(level):
        @pl.when(not_top)
        def _():
            up_copy(level).start()

        for copy in across(level):
            copy.start()

        @pl.when((level > 0) | (c == 0))
        def _():
            to_core(level, 0).start()

    def chunk(first, second, masked):
        def tiles(part, i):
            lanes = slice(i * LANES, (i + 1) * LANES)
            halves = [
                held[pl.ds(b, 2), part, :, lanes].reshape(2 * tokens, LANES)
                for b in (first, second)
            ]
            return jnp.concatenate(halves, 0)

        attend_chunk(
            q_s,
            lambda i: tiles(0, i),
            lambda i: tiles(1, i),
            acc,
            masked,
            col * tokens,
            0,
        )

    def core_arrival(level, column):
        whole(level, 5, block(level, 1 - c, column), core_dev).wait_recv()

    def from_below(level):
        whole(level, 0, block(level, c, col), down_dev).wait_recv()
        own_sends(level)

    own_sends(0)
    loads[2].wait()
    for h in range(KV):
        for p in range(PAIRS):
            q_s[h, p * tokens : (p + 1) * tokens, :] = (
                q_ref[:, (h * PAIRS + p) * LANES : (h * PAIRS + p + 1) * LANES].astype(jnp.float32)
                * 0.125
            ).astype(jnp.bfloat16)
    acc[...] = jnp.zeros_like(acc)

    def lap(level, _):
        inside = level <= z

        @pl.when(inside)
        def _():
            piece(level, 1, block(level, c, x_col), 0, x_dev).wait_recv()
            piece(level, 2, block(level, c, y_col), 1, y_dev).wait_recv()
            for copy in corner(level):
                copy.start()

        @pl.when(level < z)
        def _():
            from_below(level + 1)

        @pl.when((level > 1) | ((level == 1) & (c == 1)))
        def _():
            core_arrival(level - 1, y_col)
            core_arrival(level - 1, d_col)

            @pl.when(level == 1)
            def _():
                core_arrival(0, col)
                core_arrival(0, x_col)

            far = 2 * (1 - y)
            first = jnp.where(level == 1, block(0, 1 - c, 0), block(level - 1, c, far))
            second = jnp.where(level == 1, block(0, 1 - c, 2), block(level - 1, 1 - c, far))
            chunk(first, second, False)

        @pl.when(inside)
        def _():
            piece(level, 9, block(level, c, x_col), 1, x_dev).wait_recv()
            piece(level, 10, block(level, c, y_col), 0, y_dev).wait_recv()

            @pl.when((level > 0) | (c == 0))
            def _():
                to_core(level, 1).start()
                to_core(level, 2).start()

        @pl.when(inside & (level > 0))
        def _():
            core_arrival(level, col)
            core_arrival(level, x_col)
            chunk(block(level, c, 2 * y), block(level, 1 - c, 2 * y), False)

        @pl.when(inside)
        def _():
            b = block(level, c, d_col)
            piece(level, 3, b, 0, y_dev).wait_recv()
            piece(level, 4, b, 1, x_dev).wait_recv()

            @pl.when((level > 0) | (c == 0))
            def _():
                to_core(level, 3).start()

        @pl.when(level == 0)
        def _():
            chunk(row * cols, row * cols + 2, True)

        return 0

    lax.fori_loop(0, z + 2, lap, 0)

    for h in range(KV):
        for p in range(PAIRS):
            part = acc[h, p * tokens : (p + 1) * tokens, :]
            o_ref[:, (h * PAIRS + p) * LANES : (h * PAIRS + p + 1) * LANES] = (
                part[:, :LANES] / jnp.maximum(part[:, LANES:], 1.0)
            ).astype(jnp.bfloat16)

    def drain(level, _):
        for copy in across(level) + corner(level):
            copy.wait_send()

        @pl.when(not_top)
        def _():
            up_copy(level).wait_send()

        @pl.when((level > 0) | (c == 0))
        def _():
            for which in range(4):
                to_core(level, which).wait_send()

        return 0

    lax.fori_loop(0, z + 1, drain, 0)


def fused(shape, queries, keys, values):
    tokens, width = keys.shape
    rows, cols = shape
    in_vmem = pl.BlockSpec(memory_space=pltpu.VMEM)
    return pl.pallas_call(
        functools.partial(fused_kernel, ("row", "col"), shape),
        out_shape=jax.ShapeDtypeStruct(queries.shape, jnp.bfloat16),
        in_specs=[pl.BlockSpec(memory_space=pltpu.HBM)] * 3,
        out_specs=in_vmem,
        scratch_shapes=[
            pltpu.VMEM(queries.shape, jnp.bfloat16),
            pltpu.VMEM(keys.shape, jnp.bfloat16),
            pltpu.VMEM(values.shape, jnp.bfloat16),
            pltpu.VMEM((KV, PAIRS * tokens, LANES), jnp.bfloat16),
            pltpu.VMEM((KV, PAIRS * tokens, 2 * LANES), jnp.float32),
            pltpu.VMEM((rows * cols, 2, tokens, width), jnp.float32),
            pltpu.SemaphoreType.DMA((3,)),
            pltpu.SemaphoreType.DMA((rows // 2, 11)),
            pltpu.SemaphoreType.DMA((rows * cols, 2)),
        ],
        compiler_params=pltpu.CompilerParams(
            collective_id=0, has_side_effects=True, vmem_limit_bytes=60 * 2**20
        ),
    )(queries, keys, values)


def solution(mesh):
    placed = P(("row", "col"), None)
    rows, cols = mesh.shape["row"], mesh.shape["col"]

    def whole(queries, keys, values):
        held_bytes = keys.size * 8
        if cols == 4 and rows % 2 == 0 and held_bytes <= 16 * 2**20:
            local = functools.partial(fused, (rows, cols))
        else:
            local = on_device
        return jax.shard_map(
            local, mesh=mesh, in_specs=(placed,) * 3, out_specs=placed, check_vma=False
        )(queries, keys, values)

    return whole
```
